32 devices in a mesh: run: 2 (over x), blk: 4 (over y, core), grp: 4 (over z).
Axes of the slice: x: 2, y: 2, z: 4, core: 2. Of those that a mesh axis runs over, the one named last changes fastest.
Arguments:
- a_gate: bfloat16 [7168, 4096], P('blk', ('run', 'grp')), may hold values from -6 to 6
- a_up: bfloat16 [7168, 4096], P('blk', ('run', 'grp')), may hold values from -6 to 6
- a_down: bfloat16 [7168, 4096], P('blk', ('run', 'grp')), may hold values from -6 to 6
- b_gate: bfloat16 [14336, 4096], P(('run', 'grp'), 'blk'), may hold values from -6 to 6
- b_up: bfloat16 [14336, 4096], P(('run', 'grp'), 'blk'), may hold values from -6 to 6
- b_down: bfloat16 [14336, 4096], P(('run', 'grp'), 'blk'), may hold values from -6 to 6
Outputs:
- cost: float32 [7168, 14336], P('blk', ('run', 'grp'))
The draws below stay inside these ranges and needn't reach their ends.
All inputs are finite; a program needn't handle non-finite values.
Results may differ from the reference program's by a relative error of at most 0.0003.
Values may be sent and summed in bfloat16 or wider, within the bound.
No kernel may reach another device: no remote copies, remote signals or barrier semaphores. Data moves between devices by JAX's collectives and lax.ppermute only.
A program may use at most 192 MiB of HBM per device.

```python
import math
import jax
import jax.numpy as jnp
from jax import lax

D = 4096
FF = 14336
ROWS = 7168


def block_scale(stream_key, extent, cuts, least, high):
    def one(dim, parts):
        draws = jax.random.uniform(jax.random.fold_in(jax.random.fold_in(stream_key, 6), dim), (parts,), jnp.float32, least / len(cuts), high / len(cuts))
        return jnp.repeat(jnp.exp(draws), extent[dim] // parts).reshape((-1,) + (1,) * (len(extent) - dim - 1))

    level = one(*cuts[0])
    for cut in cuts[1:]:
        level = level * one(*cut)
    return level


def bell_draw(key, dims, scale, limit, split=(), held_as=jnp.bfloat16):
    factor_of = block_scale(key, dims, split, -0.22, 0.18) if split else 1.0
    values = jax.random.normal(key, dims, jnp.float32) * scale * factor_of
    return jnp.minimum(jnp.maximum(values, -limit), limit).astype(held_as)


def setup_inputs(seed: int = 0) -> dict:
    key_list = jax.random.split(jax.random.key(seed), 7)
    return {
        "a_gate": bell_draw(key_list[0], (ROWS, D), 1.0, 6.0, ((0, 4), (1, 8))),
        "a_up": bell_draw(key_list[1], (ROWS, D), 1.0, 6.0, ((0, 4), (1, 8))),
        "a_down": bell_draw(key_list[2], (ROWS, D), 1.0, 6.0, ((0, 4), (1, 8))),
        "b_gate": bell_draw(key_list[3], (FF, D), 1.0, 6.0, ((0, 8), (1, 4))),
        "b_up": bell_draw(key_list[4], (FF, D), 1.0, 6.0, ((0, 8), (1, 4))),
        "b_down": bell_draw(key_list[5], (FF, D), 1.0, 6.0, ((0, 8), (1, 4))),
    }


def pair_term(left, right):
    return lax.dot_general(left, right, (((1,), (1,)), ((), ())), preferred_element_type=jnp.float32)

def reference(a_gate, a_up, a_down, b_gate, b_up, b_down):
    total = pair_term(a_gate, b_gate) + pair_term(a_up, b_up) + pair_term(a_down, b_down)
    return total * (1.0 / math.sqrt(3.0 * D))
```

```python
import functools
import math

import jax
import jax.numpy as jnp
from jax import lax
from jax.experimental import pallas as pl
from jax.experimental.pallas import tpu as pltpu
from jax.sharding import PartitionSpec as P


def ring_order(n):
    return list(range(0, n, 2)) + list(range(1, n, 2))[::-1]


def ring_step(value, order, axis):
    n = len(order)
    return lax.ppermute(value, axis, [(order[i], order[(i + 1) % n]) for i in range(n)])


def shift(value, by, n, axis):
    return lax.ppermute(value, axis, [(i, (i + by) % n) for i in range(n)])


def tile(extent, most):
    return max(t for t in range(128, most + 1, 128) if extent % t == 0)


def add_terms_body(count, first, scale, cols_ref, *refs):
    lefts, rights = refs[:count], refs[count : 2 * count]
    out = refs[-1]
    total = None if first else refs[2 * count][...]
    for left, right in zip(lefts, rights):
        term = lax.dot_general(
            left[...], right[...], (((1,), (1,)), ((), ())), preferred_element_type=jnp.float32
        )
        total = term if total is None else total + term
    out[...] = total if scale is None else total * scale


def add_terms(total, pieces, scale=None):
    rows, across = pieces[0][0].shape[0], pieces[0][1].shape[0]
    tm, tn = tile(rows, 896), tile(across, 896)
    count, first = len(pieces), total is None
    in_specs = [
        pl.BlockSpec((tm, a.shape[1]), lambda i, j, cols: (i, 0)) for a, _, _ in pieces
    ] + [
        pl.BlockSpec((tn, a.shape[1]), functools.partial(lambda p, i, j, cols: (j, cols[p]), p))
        for p, (a, _, _) in enumerate(pieces)
    ]
    place = pl.BlockSpec((tm, tn), lambda i, j, cols: (i, j))
    operands = [a for a, _, _ in pieces] + [b for _, b, _ in pieces]
    if not first:
        in_specs.append(place)
        operands.append(total)
    deep = sum(a.shape[1] for a, _, _ in pieces)
    return pl.pallas_call(
        functools.partial(add_terms_body, count, first, scale),
        grid_spec=pltpu.PrefetchScalarGridSpec(
            num_scalar_prefetch=1,
            grid=(rows // tm, across // tn),
            in_specs=in_specs,
            out_specs=place,
        ),
        out_shape=jax.ShapeDtypeStruct((rows, across), jnp.float32),
        input_output_aliases={} if first else {2 * count + 1: 0},
        compiler_params=pltpu.CompilerParams(vmem_limit_bytes=48 * 1024 * 1024),
        cost_estimate=pl.CostEstimate(
            flops=2 * rows * across * deep,
            bytes_accessed=2 * deep * (rows + across) + (4 if first else 8) * rows * across,
            transcendentals=0,
        ),
    )(jnp.stack([c for _, _, c in pieces]), *operands)


def make_local(runs, grps):
    order = ring_order(grps)
    place = [order.index(i) for i in range(grps)]
    came_from = [[order[(place[g] - s) % grps] for g in range(grps)] for s in range(grps)]

    def local(a_gate, a_up, a_down, b_gate, b_up, b_down):
        depth = a_gate.shape[1]
        width = depth * runs * grps
        half = depth // 2
        run = lax.axis_index("run")
        grp = lax.axis_index("grp")
        b_full = [lax.all_gather(b, "blk", axis=1, tiled=True) for b in (b_gate, b_up, b_down)]

        def block(r, s):
            return lax.rem(run - r + runs, runs) * grps + jnp.array(came_from[s], jnp.int32)[grp]

        def ring_first(piece):
            got = []
            held = piece
            for s in range(grps):
                got.append([(held, 0, s)])
                for r in range(1, runs):
                    got[-1].append((shift(held, r, runs, "run"), r, s))
                if s < grps - 1:
                    held = ring_step(held, order, "grp")
            return got

        def run_first(piece):
            held = [piece] + [shift(piece, r, runs, "run") for r in range(1, runs)]
            got = []
            for s in range(grps):
                got.append([(h, r, s) for r, h in enumerate(held)])
                if s < grps - 1:
                    held = [ring_step(h, order, "grp") for h in held]
            return got

        gate, up = ring_first(a_gate), ring_first(a_up)
        low, high = ring_first(a_down[:, :half]), run_first(a_down[:, half:])
        calls = [[(v, b_full[0], block(r, s)) for v, r, s in g] for g in gate]
        calls += [[(v, b_full[1], block(r, s)) for v, r, s in g] for g in up]
        calls += [
            [(v, b_full[2], 2 * block(r, s)) for v, r, s in g]
            + [(v, b_full[2], 2 * block(r, s) + 1) for v, r, s in h]
            for g, h in zip(low, high)
        ]
        total = None
        for i, pieces in enumerate(calls):
            last = i == len(calls) - 1
            total = add_terms(total, pieces, 1.0 / math.sqrt(3.0 * width) if last else None)
        return total

    return local


def solution(mesh):
    placed = (
        P("blk", ("run", "grp")),
        P("blk", ("run", "grp")),
        P("blk", ("run", "grp")),
        P(("run", "grp"), "blk"),
        P(("run", "grp"), "blk"),
        P(("run", "grp"), "blk"),
    )
    local = make_local(mesh.shape["run"], mesh.shape["grp"])
    return jax.shard_map(
        local, mesh=mesh, in_specs=placed, out_specs=P("blk", ("run", "grp")), check_vma=False
    )
```

```python
import functools
import math

import jax
import jax.numpy as jnp
from jax import lax
from jax.experimental import pallas as pl
from jax.experimental.pallas import tpu as pltpu
from jax.sharding import PartitionSpec as P


def cycle_of(runs, grps):
    rows = [[r * grps + g for g in range(grps)] for r in range(runs)]
    return [i for r, row in enumerate(rows) for i in (row if r % 2 == 0 else row[::-1])]


def pass_on(value, cycle, way):
    n = len(cycle)
    pairs = [(cycle[i], cycle[(i + way) % n]) for i in range(n)]
    return lax.ppermute(value, ("run", "grp"), pairs)


def tile(extent, most):
    return max(t for t in range(128, most + 1, 128) if extent % t == 0)


def add_terms_body(count, first, scale, blocks_ref, *refs):
    lefts, rights = refs[:count], refs[count : 2 * count]
    out, mark = refs[-2:]
    mark[...] = jnp.zeros_like(mark)
    total = None if first else refs[2 * count][...]
    for left, right in zip(lefts, rights):
        term = lax.dot_general(
            left[...], right[...], (((1,), (1,)), ((), ())), preferred_element_type=jnp.float32
        )
        total = term if total is None else total + term
    out[...] = total if scale is None else total * scale


def add_terms(total, blocks, pieces, scale=None):
    rows, across = pieces[0][0].shape[0], pieces[0][1].shape[0]
    tm = tile(rows, 256)
    count, first = len(pieces), total is None

    def columns(step, parts, part, i, blocks):
        return 0, blocks[step] * parts + part

    in_specs = [pl.BlockSpec((tm, p[0].shape[1]), lambda i, blocks: (i, 0)) for p in pieces]
    in_specs += [
        pl.BlockSpec((across, p[0].shape[1]), functools.partial(columns, *p[2:])) for p in pieces
    ]
    place = pl.BlockSpec((tm, across), lambda i, blocks: (i, 0))
    operands = [p[0] for p in pieces] + [p[1] for p in pieces]
    if not first:
        in_specs.append(place)
        operands.append(total)
    deep = sum(p[0].shape[1] for p in pieces)
    return pl.pallas_call(
        functools.partial(add_terms_body, count, first, scale),
        grid_spec=pltpu.PrefetchScalarGridSpec(
            num_scalar_prefetch=1,
            grid=(rows // tm,),
            in_specs=in_specs,
            out_specs=[place, pl.BlockSpec((8, 128), lambda i, blocks: (0, 0))],
        ),
        out_shape=[
            jax.ShapeDtypeStruct((rows, across), jnp.float32),
            jax.ShapeDtypeStruct((8, 128), jnp.float32),
        ],
        input_output_aliases={} if first else {2 * count + 1: 0},
        compiler_params=pltpu.CompilerParams(vmem_limit_bytes=60 * 1024 * 1024),
        cost_estimate=pl.CostEstimate(
            flops=2 * rows * across * deep,
            bytes_accessed=2 * deep * (rows + across) + (4 if first else 8) * rows * across,
            transcendentals=0,
        ),
    )(blocks, *operands)


def make_local(runs, grps):
    cycle = cycle_of(runs, grps)
    n = len(cycle)
    source = [[cycle[(cycle.index(d) - s) % n] for s in range(n)] for d in range(n)]

    def local(a_gate, a_up, a_down, b_gate, b_up, b_down):
        depth = a_gate.shape[1]
        half = depth // 2
        here = lax.axis_index(("run", "grp"))
        blocks = jnp.array(source, jnp.int32)[here]
        b_full = [lax.all_gather(b, "blk", axis=1, tiled=True) for b in (b_gate, b_up, b_down)]

        lanes = [
            [(a_gate, 0, 1, 0), (a_down[:, :half], 2, 2, 0)],
            [(a_up, 1, 1, 0), (a_down[:, half:], 2, 2, 1)],
        ]
        rounds = n // 2
        waiting = [(a_gate, b_full[0], 0, 1, 0)]
        late = [(a_up, b_full[1], 0, 1, 0)]
        total, marks = None, [None]
        held = [None, None]
        for stage in range(2 * rounds):
            phase, s = stage // rounds, stage % rounds + 1
            if stage == rounds:
                waiting.append((a_down, b_full[2], 0, 1, 0))
            arrived = []
            for lane in range(2):
                a, tensor, parts, part = lanes[lane][phase]
                ahead, back = (a, a) if s == 1 else held[lane]
                if s == 1 and phase:
                    ahead, back, _ = lax.optimization_barrier((ahead, back, held[lane]))
                if stage > 1:
                    ahead, back, _ = lax.optimization_barrier((ahead, back, marks[stage - 1]))
                b = b_full[tensor]
                if 2 * s < n:
                    held[lane] = pass_on(ahead, cycle, 1), pass_on(back, cycle, -1)
                    arrived += [
                        (held[lane][0], b, s, parts, part),
                        (held[lane][1], b, n - s, parts, part),
                    ]
                elif parts == 1:
                    held[lane] = pass_on(ahead[:, :half], cycle, 1), pass_on(back[:, half:], cycle, -1)
                    arrived += [(held[lane][0], b, s, 2, 0), (held[lane][1], b, s, 2, 1)]
                else:
                    last_one = pass_on(back, cycle, -1) if part else pass_on(ahead, cycle, 1)
                    arrived += [(last_one, b, s, parts, part)]
            if phase == 0 and s < 3 and s < rounds:
                waiting += arrived[:2]
                late += arrived[2:]
            else:
                waiting += arrived[:2] + late + arrived[2:]
                late = []
            while waiting:
                call, deep = [], 0
                while waiting and deep + waiting[0][0].shape[1] <= 4 * depth:
                    deep += waiting[0][0].shape[1]
                    call.append(waiting.pop(0))
                last = stage == 2 * rounds - 1 and not waiting
                scale = 1.0 / math.sqrt(3.0 * depth * n) if last else None
                total, mark = add_terms(total, blocks, call, scale)
            marks.append(mark)
        return total

    return local


def solution(mesh):
    placed = (
        P("blk", ("run", "grp")),
        P("blk", ("run", "grp")),
        P("blk", ("run", "grp")),
        P(("run", "grp"), "blk"),
        P(("run", "grp"), "blk"),
        P(("run", "grp"), "blk"),
    )
    local = make_local(mesh.shape["run"], mesh.shape["grp"])
    return jax.shard_map(
        local, mesh=mesh, in_specs=placed, out_specs=P("blk", ("run", "grp")), check_vma=False
    )
```

```python
import functools
import math

import jax
import jax.numpy as jnp
from jax import lax
from jax.experimental import pallas as pl
from jax.experimental.pallas import tpu as pltpu
from jax.sharding import PartitionSpec as P


def cycle_of(runs, grps):
    rows = [[r * grps + g for g in range(grps)] for r in range(runs)]
    return [i for r, row in enumerate(rows) for i in (row if r % 2 == 0 else row[::-1])]


def pass_on(value, cycle, way):
    n = len(cycle)
    pairs = [(cycle[i], cycle[(i + way) % n]) for i in range(n)]
    return lax.ppermute(value, ("run", "grp"), pairs)


def tile(extent, most):
    return max(t for t in range(128, most + 1, 128) if extent % t == 0)


def add_terms_body(columns, first, scale, tm, blocks_ref, *refs):
    count = len(columns)
    sources = refs[: 2 * count]
    total = None if first else refs[2 * count]
    out, mark = refs[-2:]
    mark[...] = jnp.zeros_like(mark)
    rows = sources[0].shape[0]
    across = sources[count].shape[0]

    def step(*tiles):
        lefts, rights = tiles[:count], tiles[count : 2 * count]
        here = pl.ds(pl.multiple_of(pl.program_id(0) * tm, tm), tm)
        result = None if first else total[here, :]
        for left, right in zip(lefts, rights):
            term = lax.dot_general(
                left[...], right[...], (((1,), (1,)), ((), ())), preferred_element_type=jnp.float32
            )
            result = term if result is None else result + term
        if scale is None:
            out[here, :] = result
        else:
            tiles[-1][...] = result * scale

    def place(wide, which, parts, part):
        return pl.BlockSpec((across, wide), lambda i: (0, blocks_ref[which] * parts + part))

    specs = [pl.BlockSpec((tm, wide), lambda i: (i, 0)) for wide, *_ in columns]
    specs += [place(*c) for c in columns]
    result_specs = [] if scale is None else [pl.BlockSpec((tm, across), lambda i: (i, 0))]
    results = [] if scale is None else [out]
    pltpu.emit_pipeline(step, grid=(rows // tm,), in_specs=specs, out_specs=result_specs)(
        *sources, *results
    )


def add_terms(total, blocks, pieces, scale=None):
    rows, across = pieces[0][0].shape[0], pieces[0][1].shape[0]
    first, last = total is None, scale is not None
    columns = [(p[0].shape[1],) + tuple(p[2:]) for p in pieces]
    operands = [p[0] for p in pieces] + [p[1] for p in pieces]
    in_specs = [pl.BlockSpec(memory_space=pl.ANY)] * len(operands)
    if not first:
        operands.append(pltpu.with_memory_space_constraint(total, pltpu.VMEM))
        in_specs.append(pl.BlockSpec(memory_space=pltpu.VMEM))
    deep = sum(c[0] for c in columns)
    if last:
        shape = jax.ShapeDtypeStruct((rows, across), jnp.float32)
    else:
        shape = pltpu.VMEM((rows, across), jnp.float32)
    return pl.pallas_call(
        functools.partial(add_terms_body, columns, first, scale, tile(rows, 256)),
        in_specs=[pl.BlockSpec(memory_space=pltpu.SMEM)] + in_specs,
        out_specs=[
            pl.BlockSpec(memory_space=pl.ANY if last else pltpu.VMEM),
            pl.BlockSpec(memory_space=pltpu.VMEM),
        ],
        out_shape=[shape, jax.ShapeDtypeStruct((8, 128), jnp.float32)],
        input_output_aliases={} if first or last else {len(operands): 0},
        compiler_params=pltpu.CompilerParams(vmem_limit_bytes=44 * 1024 * 1024),
        cost_estimate=pl.CostEstimate(
            flops=2 * rows * across * deep,
            bytes_accessed=2 * deep * (rows + across),
            transcendentals=0,
        ),
    )(blocks, *operands)


def make_local(runs, grps):
    cycle = cycle_of(runs, grps)
    n = len(cycle)
    source = [[cycle[(cycle.index(d) - s) % n] for s in range(n)] for d in range(n)]

    def local(a_gate, a_up, a_down, b_gate, b_up, b_down):
        depth = a_gate.shape[1]
        half = depth // 2
        here = lax.axis_index(("run", "grp"))
        blocks = jnp.array(source, jnp.int32)[here]
        b_full = [lax.all_gather(b, "blk", axis=1, tiled=True) for b in (b_gate, b_up, b_down)]

        lanes = [
            [(a_gate, 0, 1, 0), (a_down[:, :half], 2, 2, 0)],
            [(a_up, 1, 1, 0), (a_down[:, half:], 2, 2, 1)],
        ]
        rounds = n // 2
        waiting = [(a_gate, b_full[0], 0, 1, 0)]
        late = [(a_up, b_full[1], 0, 1, 0)]
        total, marks = None, [None]
        held = [None, None]
        for stage in range(2 * rounds):
            phase, s = stage // rounds, stage % rounds + 1
            if stage == rounds:
                waiting.append((a_down, b_full[2], 0, 1, 0))
            arrived = []
            for lane in range(2):
                a, tensor, parts, part = lanes[lane][phase]
                ahead, back = (a, a) if s == 1 else held[lane]
                if s == 1 and phase:
                    ahead, back, _ = lax.optimization_barrier((ahead, back, held[lane]))
                if stage > 1:
                    ahead, back, _ = lax.optimization_barrier((ahead, back, marks[stage - 1]))
                b = b_full[tensor]
                if 2 * s < n:
                    held[lane] = pass_on(ahead, cycle, 1), pass_on(back, cycle, -1)
                    arrived += [
                        (held[lane][0], b, s, parts, part),
                        (held[lane][1], b, n - s, parts, part),
                    ]
                elif parts == 1:
                    held[lane] = pass_on(ahead[:, :half], cycle, 1), pass_on(back[:, half:], cycle, -1)
                    arrived += [(held[lane][0], b, s, 2, 0), (held[lane][1], b, s, 2, 1)]
                else:
                    last_one = pass_on(back, cycle, -1) if part else pass_on(ahead, cycle, 1)
                    arrived += [(last_one, b, s, parts, part)]
            if phase == 0 and s < 2 and s < rounds:
                waiting += arrived[:2]
                late += arrived[2:]
            else:
                waiting += arrived[:2] + late + arrived[2:]
                late = []
            while waiting:
                call, deep = [], 0
                while waiting and deep + waiting[0][0].shape[1] <= 4 * depth:
                    deep += waiting[0][0].shape[1]
                    call.append(waiting.pop(0))
                last = stage == 2 * rounds - 1 and not waiting
                scale = 1.0 / math.sqrt(3.0 * depth * n) if last else None
                total, mark = add_terms(total, blocks, call, scale)
            marks.append(mark)
        return total

    return local


def solution(mesh):
    placed = (
        P("blk", ("run", "grp")),
        P("blk", ("run", "grp")),
        P("blk", ("run", "grp")),
        P(("run", "grp"), "blk"),
        P(("run", "grp"), "blk"),
        P(("run", "grp"), "blk"),
    )
    local = make_local(mesh.shape["run"], mesh.shape["grp"])
    return jax.shard_map(
        local, mesh=mesh, in_specs=placed, out_specs=P("blk", ("run", "grp")), check_vma=False
    )
```

```python
import functools
import math

import jax
import jax.numpy as jnp
from jax import lax
from jax.experimental import pallas as pl
from jax.experimental.pallas import tpu as pltpu
from jax.sharding import PartitionSpec as P


def cycle_of(runs, grps):
    rows = [[r * grps + g for g in range(grps)] for r in range(runs)]
    return [i for r, row in enumerate(rows) for i in (row if r % 2 == 0 else row[::-1])]


def pass_on(value, cycle, way):
    n = len(cycle)
    pairs = [(cycle[i], cycle[(i + way) % n]) for i in range(n)]
    return lax.ppermute(value, ("run", "grp"), pairs)


def tile(extent, most):
    return max(t for t in range(16, most + 1, 16) if extent % t == 0)


def add_terms_body(groups, first, scale, blocks_ref, *refs):
    count = sum(len(columns) for _, _, columns in groups)
    mark = refs[-1]
    out = refs[-2]
    mark[...] = jnp.zeros_like(mark)
    total = None if first else refs[2 * count]
    across = refs[count].shape[0]

    def add_group(row0, rows, columns, lefts, rights):
        tm = tile(rows, 256)

        def step(*tiles):
            here = pl.ds(pl.multiple_of(row0 + pl.program_id(0) * tm, 16), tm)
            result = None if first else total[here, :]
            for left, right in zip(tiles[: len(columns)], tiles[len(columns) : 2 * len(columns)]):
                term = lax.dot_general(
                    left[...], right[...], (((1,), (1,)), ((), ())),
                    preferred_element_type=jnp.float32,
                )
                result = term if result is None else result + term
            if scale is None:
                out[here, :] = result
            else:
                tiles[-1][...] = result * scale

        def left_place(wide, start):
            return pl.BlockSpec((tm, wide), lambda i: (i + start // tm, 0))

        def right_place(wide, which, parts, part):
            return pl.BlockSpec((across, wide), lambda i: (0, blocks_ref[which] * parts + part))

        specs = [left_place(c[0], c[-1]) for c in columns]
        specs += [right_place(*c[:-1]) for c in columns]
        result_specs, results = [], []
        if scale is not None:
            result_specs = [pl.BlockSpec((tm, across), lambda i: (i + row0 // tm, 0))]
            results = [out]
        pltpu.emit_pipeline(step, grid=(rows // tm,), in_specs=specs, out_specs=result_specs)(
            *lefts, *rights, *results
        )

    at = 0
    for row0, rows, columns in groups:
        end = at + len(columns)
        add_group(row0, rows, columns, refs[at:end], refs[count + at : count + end])
        at = end


def add_terms(total, blocks, groups, scale=None, result=None):
    pieces = [p for _, _, members in groups for p in members]
    shape = pieces[0][1].shape[0] if total is None else total.shape
    first, last = total is None, scale is not None
    if first:
        shape = (groups[0][1], pieces[0][1].shape[0])
    rows, across = shape
    plan = [(row0, n, [(p[0].shape[1],) + tuple(p[2:]) for p in m]) for row0, n, m in groups]
    operands = [p[0] for p in pieces] + [p[1] for p in pieces]
    in_specs = [pl.BlockSpec(memory_space=pl.ANY)] * len(operands)
    aliases = {}
    if not first:
        operands.append(pltpu.with_memory_space_constraint(total, pltpu.VMEM))
        in_specs.append(pl.BlockSpec(memory_space=pltpu.VMEM))
        aliases = {} if last else {len(operands): 0}
    if result is not None:
        operands.append(result)
        in_specs.append(pl.BlockSpec(memory_space=pl.ANY))
        aliases = {len(operands): 0}
    work = sum(n * p[0].shape[1] for _, n, m in groups for p in m)
    return pl.pallas_call(
        functools.partial(add_terms_body, plan, first, scale),
        in_specs=[pl.BlockSpec(memory_space=pltpu.SMEM)] + in_specs,
        out_specs=[
            pl.BlockSpec(memory_space=pl.ANY if last else pltpu.VMEM),
            pl.BlockSpec(memory_space=pltpu.VMEM),
        ],
        out_shape=[
            jax.ShapeDtypeStruct(shape, jnp.float32) if last else pltpu.VMEM(shape, jnp.float32),
            jax.ShapeDtypeStruct((8, 128), jnp.float32),
        ],
        input_output_aliases=aliases,
        compiler_params=pltpu.CompilerParams(vmem_limit_bytes=44 * 1024 * 1024),
        cost_estimate=pl.CostEstimate(
            flops=2 * work * across, bytes_accessed=4 * work, transcendentals=0
        ),
    )(blocks, *operands)


def make_local(runs, grps):
    cycle = cycle_of(runs, grps)
    n = len(cycle)
    source = [[cycle[(cycle.index(d) - s) % n] for s in range(n)] for d in range(n)]

    def local(a_gate, a_up, a_down, b_gate, b_up, b_down):
        depth = a_gate.shape[1]
        half = depth // 2
        here = lax.axis_index(("run", "grp"))
        blocks = jnp.array(source, jnp.int32)[here]
        b_full = [lax.all_gather(b, "blk", axis=1, tiled=True) for b in (b_gate, b_up, b_down)]

        lanes = [
            [(a_gate, 0, 1, 0), (a_down[:, :half], 2, 2, 0)],
            [(a_up, 1, 1, 0), (a_down[:, half:], 2, 2, 1)],
        ]
        rounds = n // 2
        waiting = [(a_gate, b_full[0], 0, 1, 0)]
        late = [(a_up, b_full[1], 0, 1, 0)]
        rows = a_gate.shape[0]
        cut = rows // 4 * 3
        bands = [(0, cut), (cut, rows)]

        def by_bands(pieces):
            return [
                (start, end - start, [
                    (p[0][k],) + p[1:] + (0,) if isinstance(p[0], list) else p + (start,)
                    for p in pieces
                ])
                for k, (start, end) in enumerate(bands)
            ]

        total, marks = None, [None]
        held = [None, None]
        for stage in range(2 * rounds):
            phase, s = stage // rounds, stage % rounds + 1
            if stage == rounds:
                waiting.append((a_down, b_full[2], 0, 1, 0))
            arrived = []
            for lane in range(2):
                a, tensor, parts, part = lanes[lane][phase]
                ahead, back = (a, a) if s == 1 else held[lane]
                if s == 1 and phase:
                    ahead, back, _ = lax.optimization_barrier((ahead, back, held[lane]))
                if stage > 1:
                    ahead, back, _ = lax.optimization_barrier((ahead, back, marks[stage - 1]))
                b = b_full[tensor]
                way = -1 if part else 1
                if phase and n - 4 < 2 * s < n and n % 2 == 0:
                    onward, other = (back, ahead) if part else (ahead, back)
                    onward = [pass_on(onward[start:end], cycle, way) for start, end in bands]
                    other = pass_on(other, cycle, -way)
                    held[lane] = (other, onward) if part else (onward, other)
                    arrived += [
                        (held[lane][0], b, s, parts, part),
                        (held[lane][1], b, n - s, parts, part),
                    ]
                elif 2 * s < n:
                    held[lane] = pass_on(ahead, cycle, 1), pass_on(back, cycle, -1)
                    arrived += [
                        (held[lane][0], b, s, parts, part),
                        (held[lane][1], b, n - s, parts, part),
                    ]
                elif parts == 1:
                    held[lane] = pass_on(ahead[:, :half], cycle, 1), pass_on(back[:, half:], cycle, -1)
                    arrived += [(held[lane][0], b, s, 2, 0), (held[lane][1], b, s, 2, 1)]
                else:
                    last_ones = [pass_on(v, cycle, way) for v in (back if part else ahead)]
                    arrived += [(last_ones, b, s, parts, part)]
            if phase == 0 and s < 2 and s < rounds:
                waiting += arrived[:2]
                late += arrived[2:]
            else:
                waiting += arrived[:2] + late + arrived[2:]
                late = []
            if stage == 2 * rounds - 1:
                break
            if any(isinstance(p[0], list) for p in waiting):
                total, mark = add_terms(total, blocks, by_bands(waiting))
                waiting = []
            while waiting:
                call, deep = [], 0
                while waiting and deep + waiting[0][0].shape[1] <= 4 * depth:
                    deep += waiting[0][0].shape[1]
                    call.append(waiting.pop(0))
                call = [piece + (0,) for piece in call]
                total, mark = add_terms(total, blocks, [(0, rows, call)])
            marks.append(mark)
        scale = 1.0 / math.sqrt(3.0 * depth * n)
        result = None
        for group in by_bands(waiting):
            result, _ = add_terms(total, blocks, [group], scale, result)
        return result

    return local


def solution(mesh):
    placed = (
        P("blk", ("run", "grp")),
        P("blk", ("run", "grp")),
        P("blk", ("run", "grp")),
        P(("run", "grp"), "blk"),
        P(("run", "grp"), "blk"),
        P(("run", "grp"), "blk"),
    )
    local = make_local(mesh.shape["run"], mesh.shape["grp"])
    return jax.shard_map(
        local, mesh=mesh, in_specs=placed, out_specs=P("blk", ("run", "grp")), check_vma=False
    )
```

```python
import functools
import math

import jax
import jax.numpy as jnp
from jax import lax
from jax.experimental import pallas as pl
from jax.experimental.pallas import tpu as pltpu
from jax.sharding import PartitionSpec as P


def cycle_of(runs, grps):
    rows = [[r * grps + g for g in range(grps)] for r in range(runs)]
    return [i for r, row in enumerate(rows) for i in (row if r % 2 == 0 else row[::-1])]


def pass_on(value, cycle, way):
    n = len(cycle)
    pairs = [(cycle[i], cycle[(i + way) % n]) for i in range(n)]
    return lax.ppermute(value, ("run", "grp"), pairs)


def tile(extent, most):
    return max(t for t in range(128, most + 1, 128) if extent % t == 0)


def add_terms_body(units, first, scale, tm, blocks_ref, *refs):
    many = sum(len(wides) for wides, *_ in units)
    count = len(units)
    lefts, rights = refs[:many], refs[many : many + count]
    total = None if first else refs[many + count]
    out, mark = refs[-2:]
    mark[...] = jnp.zeros_like(mark)
    rows = lefts[0].shape[0]
    across = rights[0].shape[0]

    def step(*tiles):
        here = pl.ds(pl.multiple_of(pl.program_id(0) * tm, tm), tm)
        result = None if first else total[here, :]
        at = 0
        for (wides, *_), right in zip(units, tiles[many : many + count]):
            left = [t[...] for t in tiles[at : at + len(wides)]]
            at += len(wides)
            left = left[0] if len(left) == 1 else jnp.concatenate(left, axis=1)
            term = lax.dot_general(
                left, right[...], (((1,), (1,)), ((), ())), preferred_element_type=jnp.float32
            )
            result = term if result is None else result + term
        if scale is None:
            out[here, :] = result
        else:
            tiles[-1][...] = result * scale

    def place(wides, which, parts, part):
        wide = sum(wides)
        return pl.BlockSpec((across, wide), lambda i: (0, blocks_ref[which] * parts + part))

    specs = [pl.BlockSpec((tm, wide), lambda i: (i, 0)) for wides, *_ in units for wide in wides]
    specs += [place(*u) for u in units]
    result_specs = [] if scale is None else [pl.BlockSpec((tm, across), lambda i: (i, 0))]
    results = [] if scale is None else [out]
    pltpu.emit_pipeline(step, grid=(rows // tm,), in_specs=specs, out_specs=result_specs)(
        *lefts, *rights, *results
    )


def join_halves(pieces):
    units = {}
    for a, b, which, parts, part in pieces:
        if parts == 2 and any(p[2:] == (which, 2, 1 - part) for p in pieces):
            units.setdefault((which, 1, 0), ({}, b))[0][part] = a
        else:
            units[which, parts, part] = ({0: a}, b)
    return [([m[k] for k in sorted(m)], b) + key for key, (m, b) in units.items()]


def add_terms(total, blocks, pieces, scale=None):
    rows, across = pieces[0][0].shape[0], pieces[0][1].shape[0]
    first, last = total is None, scale is not None
    units = [u for b in dict.fromkeys(id(p[1]) for p in pieces)
             for u in join_halves([p for p in pieces if id(p[1]) == b])]
    plan = [([a.shape[1] for a in u[0]],) + tuple(u[2:]) for u in units]
    operands = [a for u in units for a in u[0]] + [u[1] for u in units]
    in_specs = [pl.BlockSpec(memory_space=pl.ANY)] * len(operands)
    if not first:
        operands.append(pltpu.with_memory_space_constraint(total, pltpu.VMEM))
        in_specs.append(pl.BlockSpec(memory_space=pltpu.VMEM))
    deep = sum(p[0].shape[1] for p in pieces)
    if last:
        shape = jax.ShapeDtypeStruct((rows, across), jnp.float32)
    else:
        shape = pltpu.VMEM((rows, across), jnp.float32)
    return pl.pallas_call(
        functools.partial(add_terms_body, plan, first, scale, tile(rows, 448 if last else 256)),
        in_specs=[pl.BlockSpec(memory_space=pltpu.SMEM)] + in_specs,
        out_specs=[
            pl.BlockSpec(memory_space=pl.ANY if last else pltpu.VMEM),
            pl.BlockSpec(memory_space=pltpu.VMEM),
        ],
        out_shape=[shape, jax.ShapeDtypeStruct((8, 128), jnp.float32)],
        input_output_aliases={} if first or last else {len(operands): 0},
        compiler_params=pltpu.CompilerParams(vmem_limit_bytes=(28 if last else 44) * 1024 * 1024),
        cost_estimate=pl.CostEstimate(
            flops=2 * rows * across * deep,
            bytes_accessed=2 * deep * (rows + across),
            transcendentals=0,
        ),
    )(blocks, *operands)


def make_local(runs, grps):
    cycle = cycle_of(runs, grps)
    n = len(cycle)
    source = [[cycle[(cycle.index(d) - s) % n] for s in range(n)] for d in range(n)]

    def local(a_gate, a_up, a_down, b_gate, b_up, b_down):
        depth = a_gate.shape[1]
        half = depth // 2
        here = lax.axis_index(("run", "grp"))
        blocks = jnp.array(source, jnp.int32)[here]
        b_full = [lax.all_gather(b, "blk", axis=1, tiled=True) for b in (b_gate, b_up, b_down)]

        lanes = [
            [(a_gate, 0, 1, 0), (a_down[:, :half], 2, 2, 0)],
            [(a_up, 1, 1, 0), (a_down[:, half:], 2, 2, 1)],
        ]
        rounds = n // 2
        waiting = [(a_gate, b_full[0], 0, 1, 0)]
        late = [(a_up, b_full[1], 0, 1, 0)]
        total, marks = None, [None]
        held = [None, None]
        for stage in range(2 * rounds):
            phase, s = stage // rounds, stage % rounds + 1
            if stage == rounds:
                waiting.append((a_down, b_full[2], 0, 1, 0))
            arrived = []
            for lane in range(2):
                a, tensor, parts, part = lanes[lane][phase]
                ahead, back = (a, a) if s == 1 else held[lane]
                if s == 1 and phase:
                    ahead, back, _ = lax.optimization_barrier((ahead, back, held[lane]))
                if stage == 2 * rounds - 1 and n % 2 == 0:
                    if part:
                        back, _ = lax.optimization_barrier((back, marks[stage - 1]))
                    else:
                        ahead, _ = lax.optimization_barrier((ahead, marks[stage - 1]))
                elif stage > 1:
                    ahead, back, _ = lax.optimization_barrier((ahead, back, marks[stage - 1]))
                b = b_full[tensor]
                if 2 * s < n:
                    held[lane] = pass_on(ahead, cycle, 1), pass_on(back, cycle, -1)
                    arrived += [
                        (held[lane][0], b, s, parts, part),
                        (held[lane][1], b, n - s, parts, part),
                    ]
                elif parts == 1:
                    held[lane] = pass_on(ahead[:, :half], cycle, 1), pass_on(back[:, half:], cycle, -1)
                    arrived += [(held[lane][0], b, s, 2, 0), (held[lane][1], b, s, 2, 1)]
                else:
                    last_one = pass_on(back, cycle, -1) if part else pass_on(ahead, cycle, 1)
                    arrived += [(last_one, b, s, parts, part)]
            if phase == 0 and s < 2 and s < rounds:
                waiting += arrived[:2]
                late += arrived[2:]
            else:
                waiting += arrived[:2] + late + arrived[2:]
                late = []
            while waiting:
                call, deep = [], 0
                while waiting and deep + waiting[0][0].shape[1] <= 4 * depth:
                    deep += waiting[0][0].shape[1]
                    call.append(waiting.pop(0))
                last = stage == 2 * rounds - 1 and not waiting
                scale = 1.0 / math.sqrt(3.0 * depth * n) if last else None
                total, mark = add_terms(total, blocks, call, scale)
            marks.append(mark)
        return total

    return local


def solution(mesh):
    placed = (
        P("blk", ("run", "grp")),
        P("blk", ("run", "grp")),
        P("blk", ("run", "grp")),
        P(("run", "grp"), "blk"),
        P(("run", "grp"), "blk"),
        P(("run", "grp"), "blk"),
    )
    local = make_local(mesh.shape["run"], mesh.shape["grp"])
    return jax.shard_map(
        local, mesh=mesh, in_specs=placed, out_specs=P("blk", ("run", "grp")), check_vma=False
    )
```

```python
import functools
import math

import jax
import jax.numpy as jnp
from jax import lax
from jax.experimental import pallas as pl
from jax.experimental.pallas import tpu as pltpu
from jax.sharding import PartitionSpec as P


def cycle_of(runs, grps):
    rows = [[r * grps + g for g in range(grps)] for r in range(runs)]
    return [i for r, row in enumerate(rows) for i in (row if r % 2 == 0 else row[::-1])]


def pass_on(value, cycle, way):
    n = len(cycle)
    pairs = [(cycle[i], cycle[(i + way) % n]) for i in range(n)]
    return lax.ppermute(value, ("run", "grp"), pairs)


def tile(extent, most):
    return max(t for t in range(128, most + 1, 128) if extent % t == 0)


def add_terms_body(units, first, scale, tm, blocks_ref, *refs):
    many = sum(len(wides) for wides, *_ in units)
    count = len(units)
    lefts, rights = refs[:many], refs[many : many + count]
    total = None if first else refs[many + count]
    out, mark = refs[-2:]
    mark[...] = jnp.zeros_like(mark)
    rows = lefts[0].shape[0]
    across = rights[0].shape[0]

    def step(*tiles):
        here = pl.ds(pl.multiple_of(pl.program_id(0) * tm, tm), tm)
        result = None if first else total[here, :]
        at = 0
        for (wides, *_), right in zip(units, tiles[many : many + count]):
            left = [t[...] for t in tiles[at : at + len(wides)]]
            at += len(wides)
            left = left[0] if len(left) == 1 else jnp.concatenate(left, axis=1)
            term = lax.dot_general(
                left, right[...], (((1,), (1,)), ((), ())), preferred_element_type=jnp.float32
            )
            result = term if result is None else result + term
        if scale is None:
            out[here, :] = result
        else:
            tiles[-1][...] = result * scale

    def place(wides, which, parts, part):
        wide = sum(wides)
        return pl.BlockSpec((across, wide), lambda i: (0, blocks_ref[which] * parts + part))

    specs = [pl.BlockSpec((tm, wide), lambda i: (i, 0)) for wides, *_ in units for wide in wides]
    specs += [place(*u) for u in units]
    result_specs = [] if scale is None else [pl.BlockSpec((tm, across), lambda i: (i, 0))]
    results = [] if scale is None else [out]
    pltpu.emit_pipeline(step, grid=(rows // tm,), in_specs=specs, out_specs=result_specs)(
        *lefts, *rights, *results
    )


def join_halves(pieces):
    units = {}
    for a, b, which, parts, part in pieces:
        if parts == 2 and any(p[2:] == (which, 2, 1 - part) for p in pieces):
            units.setdefault((which, 1, 0), ({}, b))[0][part] = a
        else:
            units[which, parts, part] = ({0: a}, b)
    return [([m[k] for k in sorted(m)], b) + key for key, (m, b) in units.items()]


def add_terms(total, blocks, pieces, scale=None):
    rows, across = pieces[0][0].shape[0], pieces[0][1].shape[0]
    first, last = total is None, scale is not None
    units = [u for b in dict.fromkeys(id(p[1]) for p in pieces)
             for u in join_halves([p for p in pieces if id(p[1]) == b])]
    plan = [([a.shape[1] for a in u[0]],) + tuple(u[2:]) for u in units]
    operands = [a for u in units for a in u[0]] + [u[1] for u in units]
    in_specs = [pl.BlockSpec(memory_space=pl.ANY)] * len(operands)
    if not first:
        operands.append(pltpu.with_memory_space_constraint(total, pltpu.VMEM))
        in_specs.append(pl.BlockSpec(memory_space=pltpu.VMEM))
    deep = sum(p[0].shape[1] for p in pieces)
    if last:
        shape = jax.ShapeDtypeStruct((rows, across), jnp.float32)
    else:
        shape = pltpu.VMEM((rows, across), jnp.float32)
    return pl.pallas_call(
        functools.partial(add_terms_body, plan, first, scale, tile(rows, 256)),
        in_specs=[pl.BlockSpec(memory_space=pltpu.SMEM)] + in_specs,
        out_specs=[
            pl.BlockSpec(memory_space=pl.ANY if last else pltpu.VMEM),
            pl.BlockSpec(memory_space=pltpu.VMEM),
        ],
        out_shape=[shape, jax.ShapeDtypeStruct((8, 128), jnp.float32)],
        input_output_aliases={} if first or last else {len(operands): 0},
        compiler_params=pltpu.CompilerParams(vmem_limit_bytes=(28 if last else 44) * 1024 * 1024),
        cost_estimate=pl.CostEstimate(
            flops=2 * rows * across * deep,
            bytes_accessed=2 * deep * (rows + across),
            transcendentals=0,
        ),
    )(blocks, *operands)


def make_local(runs, grps):
    cycle = cycle_of(runs, grps)
    n = len(cycle)
    source = [[cycle[(cycle.index(d) - s) % n] for s in range(n)] for d in range(n)]

    def local(a_gate, a_up, a_down, b_gate, b_up, b_down):
        depth = a_gate.shape[1]
        half = depth // 2
        here = lax.axis_index(("run", "grp"))
        blocks = jnp.array(source, jnp.int32)[here]
        b_full = [lax.all_gather(b, "blk", axis=1, tiled=True) for b in (b_gate, b_up, b_down)]

        lanes = [
            [(a_gate, 0, 1, 0), (a_down[:, :half], 2, 2, 0)],
            [(a_up, 1, 1, 0), (a_down[:, half:], 2, 2, 1)],
        ]
        rounds = n // 2
        waiting = [(a_gate, b_full[0], 0, 1, 0)]
        late = [(a_up, b_full[1], 0, 1, 0)]
        total, marks = None, [None]
        held = [None, None]
        for stage in range(2 * rounds):
            phase, s = stage // rounds, stage % rounds + 1
            if stage == rounds:
                waiting.append((a_down, b_full[2], 0, 1, 0))
            arrived = []
            for lane in range(2):
                a, tensor, parts, part = lanes[lane][phase]
                ahead, back = (a, a) if s == 1 else held[lane]
                if s == 1 and phase:
                    ahead, back, _ = lax.optimization_barrier((ahead, back, held[lane]))
                if stage == 2 * rounds - 1 and n % 2 == 0:
                    if part:
                        back, _ = lax.optimization_barrier((back, marks[stage - 1]))
                    else:
                        ahead, _ = lax.optimization_barrier((ahead, marks[stage - 1]))
                elif stage > 1:
                    ahead, back, _ = lax.optimization_barrier((ahead, back, marks[stage - 1]))
                b = b_full[tensor]
                if 2 * s < n:
                    held[lane] = pass_on(ahead, cycle, 1), pass_on(back, cycle, -1)
                    arrived += [
                        (held[lane][0], b, s, parts, part),
                        (held[lane][1], b, n - s, parts, part),
                    ]
                elif parts == 1:
                    held[lane] = pass_on(ahead[:, :half], cycle, 1), pass_on(back[:, half:], cycle, -1)
                    arrived += [(held[lane][0], b, s, 2, 0), (held[lane][1], b, s, 2, 1)]
                else:
                    last_one = pass_on(back, cycle, -1) if part else pass_on(ahead, cycle, 1)
                    arrived += [(last_one, b, s, parts, part)]
            if phase == 0 and s < 2 and s < rounds:
                waiting += arrived[:2]
                late += arrived[2:]
            else:
                waiting += arrived[:2] + late + arrived[2:]
                late = []
            while waiting:
                call, deep = [], 0
                while waiting and deep + waiting[0][0].shape[1] <= 4 * depth:
                    deep += waiting[0][0].shape[1]
                    call.append(waiting.pop(0))
                last = stage == 2 * rounds - 1 and not waiting
                scale = 1.0 / math.sqrt(3.0 * depth * n) if last else None
                total, mark = add_terms(total, blocks, call, scale)
            marks.append(mark)
        return total

    return local


def solution(mesh):
    placed = (
        P("blk", ("run", "grp")),
        P("blk", ("run", "grp")),
        P("blk", ("run", "grp")),
        P(("run", "grp"), "blk"),
        P(("run", "grp"), "blk"),
        P(("run", "grp"), "blk"),
    )
    local = make_local(mesh.shape["run"], mesh.shape["grp"])
    return jax.shard_map(
        local, mesh=mesh, in_specs=placed, out_specs=P("blk", ("run", "grp")), check_vma=False
    )
```

```python
import functools
import math

import jax
import jax.numpy as jnp
from jax import lax
from jax.experimental import pallas as pl
from jax.experimental.pallas import tpu as pltpu
from jax.sharding import PartitionSpec as P


def cycle_of(runs, grps):
    rows = [[r * grps + g for g in range(grps)] for r in range(runs)]
    return [i for r, row in enumerate(rows) for i in (row if r % 2 == 0 else row[::-1])]


def pass_on(value, cycle, way):
    n = len(cycle)
    pairs = [(cycle[i], cycle[(i + way) % n]) for i in range(n)]
    return lax.ppermute(value, ("run", "grp"), pairs)


def tile(extent, most):
    return max(t for t in range(128, most + 1, 128) if extent % t == 0)


def add_terms_body(units, first, scale, tm, blocks_ref, *refs):
    many = sum(len(wides) for wides, *_ in units)
    count = len(units)
    lefts, rights = refs[:many], refs[many : many + count]
    total = None if first else refs[many + count]
    out, mark = refs[-2:]
    mark[...] = jnp.zeros_like(mark)
    rows = lefts[0].shape[0]
    across = rights[0].shape[0]

    def step(*tiles):
        here = pl.ds(pl.multiple_of(pl.program_id(0) * tm, tm), tm)
        if scale is None:
            result = None if first else total[here, :]
        else:
            result = total[:, here]
        at = 0
        for (wides, *_), right in zip(units, tiles[many : many + count]):
            left = [t[...] for t in tiles[at : at + len(wides)]]
            at += len(wides)
            left = left[0] if len(left) == 1 else jnp.concatenate(left, axis=1)
            term = lax.dot_general(
                left, right[...], (((1,), (1,)), ((), ())), preferred_element_type=jnp.float32
            )
            result = term if result is None else result + term
        if scale is None:
            out[here, :] = result
        else:
            tiles[-1][...] = result * scale

    def place(wides, which, parts, part):
        wide = sum(wides)
        if scale is not None:
            return pl.BlockSpec((tm, wide), lambda i: (i, blocks_ref[which] * parts + part))
        return pl.BlockSpec((across, wide), lambda i: (0, blocks_ref[which] * parts + part))

    all_wides = [wide for wides, *_ in units for wide in wides]
    if scale is None:
        specs = [pl.BlockSpec((tm, wide), lambda i: (i, 0)) for wide in all_wides]
        steps = rows // tm
    else:
        specs = [pl.BlockSpec((rows, wide), lambda i: (0, 0)) for wide in all_wides]
        steps = across // tm
    specs += [place(*u) for u in units]
    result_specs = [] if scale is None else [pl.BlockSpec((rows, tm), lambda i: (0, i))]
    results = [] if scale is None else [out]
    pltpu.emit_pipeline(step, grid=(steps,), in_specs=specs, out_specs=result_specs)(
        *lefts, *rights, *results
    )


def join_halves(pieces):
    units = {}
    for a, b, which, parts, part in pieces:
        if parts == 2 and any(p[2:] == (which, 2, 1 - part) for p in pieces):
            units.setdefault((which, 1, 0), ({}, b))[0][part] = a
        else:
            units[which, parts, part] = ({0: a}, b)
    return [([m[k] for k in sorted(m)], b) + key for key, (m, b) in units.items()]


def add_terms(total, blocks, pieces, scale=None):
    rows, across = pieces[0][0].shape[0], pieces[0][1].shape[0]
    first, last = total is None, scale is not None
    units = [u for b in dict.fromkeys(id(p[1]) for p in pieces)
             for u in join_halves([p for p in pieces if id(p[1]) == b])]
    plan = [([a.shape[1] for a in u[0]],) + tuple(u[2:]) for u in units]
    operands = [a for u in units for a in u[0]] + [u[1] for u in units]
    in_specs = [pl.BlockSpec(memory_space=pl.ANY)] * len(operands)
    if not first:
        operands.append(pltpu.with_memory_space_constraint(total, pltpu.VMEM))
        in_specs.append(pl.BlockSpec(memory_space=pltpu.VMEM))
    deep = sum(p[0].shape[1] for p in pieces)
    if last:
        shape = jax.ShapeDtypeStruct((rows, across), jnp.float32)
    else:
        shape = pltpu.VMEM((rows, across), jnp.float32)
    return pl.pallas_call(
        functools.partial(add_terms_body, plan, first, scale, tile(across if last else rows, 256)),
        in_specs=[pl.BlockSpec(memory_space=pltpu.SMEM)] + in_specs,
        out_specs=[
            pl.BlockSpec(memory_space=pl.ANY if last else pltpu.VMEM),
            pl.BlockSpec(memory_space=pltpu.VMEM),
        ],
        out_shape=[shape, jax.ShapeDtypeStruct((8, 128), jnp.float32)],
        input_output_aliases={} if first or last else {len(operands): 0},
        compiler_params=pltpu.CompilerParams(vmem_limit_bytes=(28 if last else 44) * 1024 * 1024),
        cost_estimate=pl.CostEstimate(
            flops=2 * rows * across * deep,
            bytes_accessed=2 * deep * (rows + across),
            transcendentals=0,
        ),
    )(blocks, *operands)


def make_local(runs, grps):
    cycle = cycle_of(runs, grps)
    n = len(cycle)
    source = [[cycle[(cycle.index(d) - s) % n] for s in range(n)] for d in range(n)]

    def local(a_gate, a_up, a_down, b_gate, b_up, b_down):
        depth = a_gate.shape[1]
        half = depth // 2
        here = lax.axis_index(("run", "grp"))
        blocks = jnp.array(source, jnp.int32)[here]
        b_full = [lax.all_gather(b, "blk", axis=1, tiled=True) for b in (b_gate, b_up, b_down)]

        lanes = [
            [(a_gate, 0, 1, 0), (a_down[:, :half], 2, 2, 0)],
            [(a_up, 1, 1, 0), (a_down[:, half:], 2, 2, 1)],
        ]
        rounds = n // 2
        waiting = [(a_gate, b_full[0], 0, 1, 0)]
        late = [(a_up, b_full[1], 0, 1, 0)]
        total, marks = None, [None]
        held = [None, None]
        for stage in range(2 * rounds):
            phase, s = stage // rounds, stage % rounds + 1
            if stage == rounds:
                waiting.append((a_down, b_full[2], 0, 1, 0))
            arrived = []
            for lane in range(2):
                a, tensor, parts, part = lanes[lane][phase]
                ahead, back = (a, a) if s == 1 else held[lane]
                if s == 1 and phase:
                    ahead, back, _ = lax.optimization_barrier((ahead, back, held[lane]))
                if stage == 2 * rounds - 1 and n % 2 == 0:
                    if part:
                        back, _ = lax.optimization_barrier((back, marks[stage - 1]))
                    else:
                        ahead, _ = lax.optimization_barrier((ahead, marks[stage - 1]))
                elif stage > 1:
                    ahead, back, _ = lax.optimization_barrier((ahead, back, marks[stage - 1]))
                b = b_full[tensor]
                if 2 * s < n:
                    held[lane] = pass_on(ahead, cycle, 1), pass_on(back, cycle, -1)
                    arrived += [
                        (held[lane][0], b, s, parts, part),
                        (held[lane][1], b, n - s, parts, part),
                    ]
                elif parts == 1:
                    held[lane] = pass_on(ahead[:, :half], cycle, 1), pass_on(back[:, half:], cycle, -1)
                    arrived += [(held[lane][0], b, s, 2, 0), (held[lane][1], b, s, 2, 1)]
                else:
                    last_one = pass_on(back, cycle, -1) if part else pass_on(ahead, cycle, 1)
                    arrived += [(last_one, b, s, parts, part)]
            if phase == 0 and s < 2 and s < rounds:
                waiting += arrived[:2]
                late += arrived[2:]
            else:
                waiting += arrived[:2] + late + arrived[2:]
                late = []
            while waiting:
                call, deep = [], 0
                while waiting and deep + waiting[0][0].shape[1] <= 4 * depth:
                    deep += waiting[0][0].shape[1]
                    call.append(waiting.pop(0))
                last = stage == 2 * rounds - 1 and not waiting
                scale = 1.0 / math.sqrt(3.0 * depth * n) if last else None
                total, mark = add_terms(total, blocks, call, scale)
            marks.append(mark)
        return total

    return local


def solution(mesh):
    placed = (
        P("blk", ("run", "grp")),
        P("blk", ("run", "grp")),
        P("blk", ("run", "grp")),
        P(("run", "grp"), "blk"),
        P(("run", "grp"), "blk"),
        P(("run", "grp"), "blk"),
    )
    local = make_local(mesh.shape["run"], mesh.shape["grp"])
    return jax.shard_map(
        local, mesh=mesh, in_specs=placed, out_specs=P("blk", ("run", "grp")), check_vma=False
    )
```
